32 devices in a mesh: seq: 8 (over y, x, core), head: 4 (over z).
Axes of the slice: x: 2, y: 2, z: 4, core: 2. Of those that a mesh axis runs over, the one named last changes fastest.
Arguments:
- row_queries: bfloat16 [8192, 2048], P('seq', 'head'), may hold values from -200 to 200
- row_keys: bfloat16 [8192, 2048], P('seq', 'head'), may hold values from -6 to 6
- row_values: bfloat16 [8192, 2048], P('seq', 'head'), may hold values from -6 to 6
- residual_in: bfloat16 [8192, 4096], P(('seq', 'head')), may hold values from -6 to 6
- out_weight: bfloat16 [2048, 4096], P('head', 'seq'), may hold values from -0.25 to 0.25
- norm_gain: float32 [4096], replicated, may hold values from 0.1 to 1.9
- qkv_weight: bfloat16 [4096, 16, 3, 128], P('seq', 'head'), may hold values from -4 to 4
Outputs:
- residual_out: bfloat16 [8192, 4096], P(('seq', 'head'))
- column_out: bfloat16 [8192, 2048], P('seq', 'head')
The draws below stay inside these ranges and needn't reach their ends.
All inputs are finite; a program needn't handle non-finite values.
Results may differ from the reference program's by a relative error of at most 0.0091.
Values may be sent and summed in bfloat16 or wider, within the bound.
No kernel may reach another device: no remote copies, remote signals or barrier semaphores. Data moves between devices by JAX's collectives and lax.ppermute only.
A program may use at most 128 MiB of HBM per device.

```python
import jax
import jax.numpy as jnp
from jax import lax

D = 4096
HEADS = 16
HD = 128
COLS = 512
TOKENS = 8192


def shared_keys(key):
    return jnp.clip(jax.random.normal(key, (TOKENS, HEADS * HD), jnp.float32), -6.0, 6.0)


def draw_row_keys(key, part):
    return shared_keys(key).astype(jnp.bfloat16)


def draw_row_queries(key, part):
    key = jax.random.fold_in(key, 11)
    first = jax.random.fold_in(key, 0)
    result = jnp.clip(jax.random.normal(first, (TOKENS, HEADS * HD), jnp.float32), -6.0, 6.0) * 2.0
    return result.astype(jnp.bfloat16)


def draw_qkv_weight(key, part):
    key = jax.random.fold_in(key, 5)
    first = jax.random.fold_in(key, 0)
    weights = jnp.clip(jax.random.normal(first, (D, HEADS, 3, HD), jnp.float32), -6.0, 6.0) * D ** (-0.5)
    return weights.astype(jnp.bfloat16)


def levels(stream_key, extent, cuts, low, top_value):
    def one(position, blocks):
        draws = jax.random.uniform(jax.random.fold_in(jax.random.fold_in(stream_key, 6), position), (blocks,), jnp.float32, low / len(cuts), top_value / len(cuts))
        return jnp.repeat(jnp.exp(draws), extent[position] // blocks).reshape((-1,) + (1,) * (len(extent) - position - 1))

    factor_of = one(*cuts[0])
    for cut in cuts[1:]:
        factor_of = factor_of * one(*cut)
    return factor_of


def normal_values(rng, shape, deviation, bound, shards=(), held_as=jnp.bfloat16):
    array = deviation * jax.random.normal(rng, shape, jnp.float32)
    if shards:
        array = array * levels(rng, shape, shards, -0.22, 0.18)
    return jnp.clip(array, -bound, bound).astype(held_as)


def setup_inputs(seed: int = 0) -> dict:
    key_of = jax.random.split(jax.random.key(seed), 8)
    return {
        "row_queries": draw_row_queries(jax.random.fold_in(key_of[7], 71), 0),
        "row_keys": draw_row_keys(jax.random.fold_in(key_of[7], 71), 0),
        "row_values": normal_values(key_of[2], (TOKENS, HEADS * HD), 1.0, 6.0, ((0, 8), (1, 4))),
        "residual_in": normal_values(key_of[3], (TOKENS, D), 1.0, 6.0, ((0, 32),)),
        "out_weight": normal_values(key_of[4], (HEADS * HD, D), (4 * HD) ** -0.5, 0.25, ((0, 4), (1, 8))),
        "norm_gain": jnp.clip(1.0 + 0.18 * jax.random.normal(key_of[5], (D,), jnp.float32), 0.1, 1.9),
        "qkv_weight": draw_qkv_weight(jax.random.fold_in(key_of[7], 71), 0),
    }


epsilon = 1e-05

def band_attention(queries, keys, values, has_prev):
    width = queries.shape[0]
    scores = jnp.einsum('qhd,khd->hqk', queries.astype(jnp.float32), keys.astype(jnp.float32)) * queries.shape[-1] ** (-0.5)
    query_col = jnp.arange(width, dtype=jnp.int32)[:, None]
    key_col = jnp.arange(2 * width, dtype=jnp.int32)[None, :]
    allowed = jnp.where(key_col < width, (key_col > query_col) & has_prev, key_col - width <= query_col)
    scores = jnp.where(allowed[None], scores, -jnp.inf)
    shifted = jnp.exp(scores - lax.optimization_barrier(jnp.max(scores, -1, keepdims=True)))
    weights = (shifted / lax.optimization_barrier(jnp.sum(shifted, -1, keepdims=True))).astype(jnp.bfloat16)
    return jnp.einsum('hqk,khd->qhd', weights.astype(jnp.float32), values.astype(jnp.float32)).astype(jnp.bfloat16)

def column_head(block):
    queries = block[:, :, 0].astype(jnp.float32)
    keys = block[:, :, 1].astype(jnp.float32)
    values = block[:, :, 2].astype(jnp.float32)
    scores = jnp.einsum('rcd,scd->crs', queries, keys) * queries.shape[-1] ** (-0.5)
    height = block.shape[0]
    allowed = jnp.arange(height, dtype=jnp.int32)[None, :] <= jnp.arange(height, dtype=jnp.int32)[:, None]
    scores = jnp.where(allowed[None], scores, -jnp.inf)
    shifted = jnp.exp(scores - lax.optimization_barrier(jnp.max(scores, -1, keepdims=True)))
    weights = (shifted / lax.optimization_barrier(jnp.sum(shifted, -1, keepdims=True))).astype(jnp.bfloat16)
    return jnp.einsum('crs,scd->rcd', weights.astype(jnp.float32), values).astype(jnp.bfloat16)

def reference(row_queries, row_keys, row_values, residual_in, out_weight, norm_gain, qkv_weight):
    grid_rows = TOKENS // COLS
    shape = (grid_rows, COLS, HEADS, HD)
    queries = row_queries.reshape(shape)
    keys = row_keys.reshape(shape)
    values = row_values.reshape(shape)
    keys_prev = jnp.concatenate([jnp.zeros_like(keys[:1]), keys[:-1]], 0)
    values_prev = jnp.concatenate([jnp.zeros_like(values[:1]), values[:-1]], 0)
    row_index = jnp.arange(grid_rows, dtype=jnp.int32)

    def one_row(item):
        query_row, key_row, value_row, key_back, value_back, number = item
        return band_attention(query_row, jnp.concatenate([key_back, key_row], 0), jnp.concatenate([value_back, value_row], 0), number > 0)
    row_out = lax.map(one_row, (queries, keys, values, keys_prev, values_prev, row_index)).reshape(TOKENS, HEADS * HD)
    projected = jnp.dot(row_out, out_weight, preferred_element_type=jnp.float32)
    residual_out = (residual_in.astype(jnp.float32) + projected).astype(jnp.bfloat16)
    stream = residual_out.astype(jnp.float32)
    center = stream - lax.optimization_barrier(jnp.mean(stream, -1, keepdims=True))
    variance = lax.optimization_barrier(jnp.mean(center * center, -1, keepdims=True))
    normed = (center * lax.rsqrt(variance + epsilon) * norm_gain).astype(jnp.bfloat16)
    column_qkv = jnp.dot(normed, qkv_weight.reshape(D, HEADS * 3 * HD), preferred_element_type=jnp.float32).astype(jnp.bfloat16)
    column_qkv = column_qkv.reshape(grid_rows, COLS, HEADS, 3, HD)
    per_head = lax.map(column_head, jnp.moveaxis(column_qkv, 2, 0))
    column_out = jnp.moveaxis(per_head, 0, 2).reshape(TOKENS, HEADS * HD)
    return (residual_out, column_out)
```

```python
import functools

import jax
import jax.numpy as jnp
from jax import lax
from jax.experimental import pallas as pl
from jax.experimental.pallas import tpu as pltpu
from jax.sharding import PartitionSpec as P

HD = 128
COLS = 512
EPSILON = 1e-05
TILE = 256
EXP2_SCALE = HD ** (-0.5) * 1.4426950408889634
MASKED = -1e30
VMEM = 56 * 1024 * 1024


def params(grid_rank):
    return pltpu.CompilerParams(
        dimension_semantics=("arbitrary",) * grid_rank, vmem_limit_bytes=VMEM
    )


def softmax_values(scores, values):
    top = jnp.max(scores, -1, keepdims=True)
    shifted = jnp.exp2((scores - top) * EXP2_SCALE)
    total = jnp.sum(shifted, -1, keepdims=True)
    summed = jnp.dot(shifted.astype(jnp.bfloat16), values, preferred_element_type=jnp.float32)
    return (summed / total).astype(jnp.bfloat16)


def scores_of(queries, keys):
    return lax.dot_general(
        queries, keys, (((1,), (1,)), ((), ())), preferred_element_type=jnp.float32
    )


def band_kernel(first_ref, q_ref, kp_ref, kc_ref, vp_ref, vc_ref, o_ref):
    has_prev = first_ref[0] + pl.program_id(0) > 0
    for tile in range(COLS // TILE):
        low, high = tile * TILE, (tile + 1) * TILE
        queries = q_ref[low:high, :]
        keys = jnp.concatenate([kp_ref[low:, :], kc_ref[:high, :]], 0)
        values = jnp.concatenate([vp_ref[low:, :], vc_ref[:high, :]], 0)
        scores = scores_of(queries, keys)
        row = lax.broadcasted_iota(jnp.int32, scores.shape, 0)
        col = lax.broadcasted_iota(jnp.int32, scores.shape, 1)
        allowed = (col > row) & (col <= row + COLS) & ((col >= COLS - low) | has_prev)
        scores = jnp.where(allowed, scores, MASKED)
        o_ref[low:high, :] = softmax_values(scores, values)


def band_attention(first, queries, key_prev, key_now, value_prev, value_now, lines, q_at, prev_at, now_at):
    groups = queries.shape[1] // HD

    def block(at):
        return pl.BlockSpec((COLS, HD), lambda line, head, _: (line + at, head))

    return pl.pallas_call(
        band_kernel,
        grid_spec=pltpu.PrefetchScalarGridSpec(
            num_scalar_prefetch=1,
            grid=(lines, groups),
            in_specs=[block(q_at), block(prev_at), block(now_at), block(prev_at), block(now_at)],
            out_specs=block(0),
        ),
        out_shape=jax.ShapeDtypeStruct((lines * COLS, groups * HD), jnp.bfloat16),
        compiler_params=params(2),
        cost_estimate=pl.CostEstimate(
            flops=4 * lines * COLS * 768 * HD * groups,
            bytes_accessed=lines * COLS * groups * HD * 12,
            transcendentals=lines * COLS * 768 * groups,
        ),
        name="band_attention",
    )(first, queries, key_prev, key_now, value_prev, value_now)


def project_kernel(parts, width, *refs):
    row_refs, (own_ref, far_ref, residual_ref, gain_ref, out_ref, normed_ref) = (
        refs[:parts],
        refs[parts:],
    )
    step = pl.program_id(0)
    terms = residual_ref[...].astype(jnp.float32)
    for part in range(parts):
        weight = own_ref[0] if part == 0 else far_ref[0, part - 1]
        terms += jnp.dot(row_refs[part][...], weight, preferred_element_type=jnp.float32)
    out_ref[:, pl.ds(pl.multiple_of(step * width, width), width)] = terms.astype(jnp.bfloat16)

    @pl.when(step == pl.num_programs(0) - 1)
    def _():
        rows = out_ref.shape[0]
        tile = min(rows, 64)

        def norm(at, _):
            here = pl.ds(pl.multiple_of(at * tile, tile), tile)
            stream = out_ref[here, :].astype(jnp.float32)
            center = stream - jnp.mean(stream, -1, keepdims=True)
            variance = jnp.mean(center * center, -1, keepdims=True)
            normed_ref[here, :] = (
                center * lax.rsqrt(variance + EPSILON) * gain_ref[...]
            ).astype(jnp.bfloat16)
            return 0

        lax.fori_loop(0, rows // tile, norm, 0)


def project_and_norm(row_parts, own_weight, far_weight, residual, gain):
    steps, depth, width = own_weight.shape
    parts = len(row_parts)
    rows, features = residual.shape
    whole = pl.BlockSpec((rows, features), lambda i: (0, 0))
    return pl.pallas_call(
        functools.partial(project_kernel, parts, width),
        grid=(steps,),
        in_specs=[pl.BlockSpec((rows, depth), lambda i: (0, 0))] * parts
        + [
            pl.BlockSpec((1, depth, width), lambda i: (i, 0, 0)),
            pl.BlockSpec((1, parts - 1, depth, width), lambda i: (i, 0, 0, 0)),
            pl.BlockSpec((rows, width), lambda i: (0, i)),
            pl.BlockSpec((1, features), lambda i: (0, 0)),
        ],
        out_specs=[whole, whole],
        out_shape=[jax.ShapeDtypeStruct((rows, features), jnp.bfloat16)] * 2,
        compiler_params=params(1),
        cost_estimate=pl.CostEstimate(
            flops=2 * rows * parts * depth * features,
            bytes_accessed=2 * parts * own_weight.size + 6 * rows * features,
            transcendentals=rows,
        ),
        name="project_and_norm",
    )(*row_parts, own_weight, far_weight, residual, gain)


def column_kernel(columns, qkv_ref, o_ref):
    height = qkv_ref.shape[0] // columns
    part = min(qkv_ref.shape[0], 256)
    for low in range(0, height * columns, part):
        high = low + part
        scores = scores_of(qkv_ref[low:high, :HD], qkv_ref[:high, HD : 2 * HD])
        row = lax.broadcasted_iota(jnp.int32, scores.shape, 0) + low
        col = lax.broadcasted_iota(jnp.int32, scores.shape, 1)
        allowed = (col <= row) & (((row - col) & (columns - 1)) == 0)
        scores = jnp.where(allowed, scores, MASKED)
        o_ref[low:high] = softmax_values(scores, qkv_ref[:high, 2 * HD :])


def column_attention(qkv):
    height, columns, features = qkv.shape
    groups = features // (3 * HD)
    attended = pl.pallas_call(
        functools.partial(column_kernel, columns),
        grid=(groups,),
        in_specs=[pl.BlockSpec((height * columns, 3 * HD), lambda g: (0, g))],
        out_specs=pl.BlockSpec((height * columns, HD), lambda g: (0, g)),
        out_shape=jax.ShapeDtypeStruct((height * columns, groups * HD), jnp.bfloat16),
        compiler_params=params(1),
        cost_estimate=pl.CostEstimate(
            flops=4 * height * columns * groups * 256 * HD,
            bytes_accessed=8 * height * columns * groups * HD,
            transcendentals=height * columns * groups * 256,
        ),
        name="column_attention",
    )(qkv.reshape(height * columns, features))
    return attended.reshape(height, columns, groups * HD)


def passed_along(array, axis, by):
    size = lax.axis_size(axis)
    pairs = [(i, i + by) for i in range(size) if 0 <= i + by < size]
    return lax.ppermute(array, axis, pairs)


def moved(value, pairs):
    return lax.ppermute(value, "head", pairs)


def line_first(array):
    return moved(array, [(0, 1), (1, 2), (2, 3)]), moved(array, [(1, 0), (2, 1), (3, 2)])


def line_second(array, below, above):
    place = lax.axis_index("head")
    at_end = (place == 0) | (place == 3)
    below_two = moved(below, [(1, 2), (2, 3)])
    above_two = moved(above, [(2, 1), (1, 0)])
    across = moved(array, [(0, 3), (3, 0)])
    slots = [
        (below, (place + 3) % 4),
        (above, (place + 1) % 4),
        (jnp.where(place < 2, above_two, below_two), (place + 2) % 4),
        (jnp.where(at_end, across, array), jnp.where(at_end, 3 - place, place)),
    ]
    gathered = lax.dynamic_update_index_in_dim(
        jnp.zeros((4, *array.shape), array.dtype), array, place, 0
    )
    for value, slot in slots:
        gathered = lax.dynamic_update_index_in_dim(gathered, value, slot, 0)
    return gathered


def from_behind(array, by):
    size = lax.axis_size("head")
    return moved(array, [(i, (i + by) % size) for i in range(size)])


def after(value, *others):
    return lax.optimization_barrier((value, *others))[0]


def per_device(row_queries, row_keys, row_values, residual_in, out_weight, norm_gain, qkv_weight):
    positions, features = row_queries.shape
    lines = positions // COLS
    seq, heads = lax.axis_size("seq"), lax.axis_size("head")
    place = lax.axis_index("head")
    share, model = residual_in.shape
    gain = norm_gain.reshape(1, model)
    block = min(share, COLS)
    blocks = COLS // block
    quarter = share // 4
    late = 3

    own_weight = lax.all_gather(out_weight, "seq")
    far_weight = [from_behind(out_weight, by) for by in range(1, heads)]
    key_back, value_back = passed_along((row_keys[-COLS:], row_values[-COLS:]), "seq", 1)
    residual = residual_in.reshape(share // block, 4, block // 4, model)
    residual_own = residual[:, 0].reshape(quarter, model)
    residual_first = jnp.stack([residual_own] * heads)
    for by in range(1, heads):
        residual_first = lax.dynamic_update_index_in_dim(
            residual_first, from_behind(residual_own, by), (place + heads - by) % heads, 0
        )
    residual_first = residual_first.reshape(heads * quarter, model)

    first_row = (lax.axis_index("seq") * lines).reshape(1)
    row_out = []
    if lines > 1:
        row_out.append(
            band_attention(
                first_row + 1,
                row_queries,
                row_keys,
                row_keys,
                row_values,
                row_values,
                lines - 1,
                1,
                0,
                1,
            )
        )
    row_out.insert(
        0,
        band_attention(
            first_row, row_queries, key_back, row_keys, value_back, row_values, 1, 0, 0, 0
        ),
    )
    row_out = jnp.concatenate(row_out, 0)
    far_weight = lax.all_gather(after(jnp.stack(far_weight), row_out), "seq")

    row_out = row_out.reshape(heads, share // block, 4, block // 4, features)
    row_first = row_out[:, :, 0].reshape(heads * quarter, features)
    row_late = row_out[:, :, 1:].reshape(heads, late * quarter, features)
    parts_first = [row_first] + [from_behind(row_first, by) for by in range(1, heads)]
    parts_late = [
        from_behind(
            lax.dynamic_index_in_dim(row_late, (place + by) % heads, 0, keepdims=False), by
        )
        if by
        else lax.dynamic_index_in_dim(row_late, place, 0, keepdims=False)
        for by in range(heads)
    ]
    qkv_own = after(qkv_weight.reshape(qkv_weight.shape[0], -1), *parts_late)
    qkv_flat = lax.all_gather(qkv_own, "seq", axis=0, tiled=True)

    out_late, normed_own = project_and_norm(
        parts_late, own_weight, far_weight, residual[:, 1:].reshape(late * quarter, model), gain
    )
    normed_own = normed_own.reshape(share // block, late, block // 4, model)
    normed_own = [normed_own[:, low:high].reshape(-1, model) for low, high in ((0, 2), (2, 3))]
    copies = [line_first(piece) for piece in normed_own]
    out_first, normed_first = project_and_norm(
        parts_first, own_weight, far_weight, residual_first, gain
    )
    out_first = lax.dynamic_slice_in_dim(out_first, place * quarter, quarter, 0)
    normed = [
        line_second(piece, *first).reshape(-1, model) for piece, first in zip(normed_own, copies)
    ]
    normed.insert(0, after(normed_first, normed[0], *copies[1]))

    def project(normed):
        own_columns = normed.shape[0] // (lines * seq)
        projected = jnp.dot(normed, qkv_flat, preferred_element_type=jnp.float32)
        qkv = projected.astype(jnp.bfloat16).reshape(lines, seq, own_columns, -1)
        return qkv.transpose(1, 0, 2, 3)

    def swap(pieces):
        return lax.all_to_all(pieces, "seq", split_axis=0, concat_axis=0, tiled=True)

    def attend(qkv):
        return column_attention(qkv.reshape(seq * lines, *qkv.shape[2:]))

    def send_back(attended):
        own_columns = attended.shape[1]
        attended = swap(attended.reshape(seq, lines, own_columns, features))
        return attended.transpose(1, 0, 2, 3).reshape(
            lines, blocks, seq * own_columns // blocks, features
        )

    qkv_first = swap(project(normed[0]))
    qkv_next = project(normed[1])
    qkv_end = project(after(normed[2], qkv_first, qkv_next))
    qkv_next = swap(qkv_next)
    sent = [send_back(attend(qkv_first))]
    qkv_end = swap(after(qkv_end, qkv_next, *sent))
    sent += [send_back(attend(qkv_next)), send_back(attend(qkv_end))]
    column_out = jnp.concatenate(sent, 2)
    residual_out = jnp.concatenate(
        [
            out_first.reshape(share // block, 1, block // 4, model),
            out_late.reshape(share // block, late, block // 4, model),
        ],
        1,
    )
    return residual_out.reshape(share, model), column_out.reshape(positions, features)


def solution(mesh):
    placed = (
        P("seq", "head"),
        P("seq", "head"),
        P("seq", "head"),
        P(("seq", "head"), None),
        P("head", "seq"),
        P(),
        P("seq", "head", None, None),
    )
    return jax.shard_map(
        per_device,
        mesh=mesh,
        in_specs=placed,
        out_specs=(P(("seq", "head"), None), P("seq", "head")),
        check_vma=False,
    )
```

```python
import functools

import jax
import jax.numpy as jnp
from jax import lax
from jax.experimental import pallas as pl
from jax.experimental.pallas import tpu as pltpu
from jax.sharding import PartitionSpec as P

HD = 128
COLS = 512
EPSILON = 1e-05
TILE = 256
EXP2_SCALE = HD ** (-0.5) * 1.4426950408889634
MASKED = -1e30
VMEM = 56 * 1024 * 1024


def params(grid_rank):
    return pltpu.CompilerParams(
        dimension_semantics=("arbitrary",) * grid_rank, vmem_limit_bytes=VMEM
    )


def softmax_values(scores, values):
    top = jnp.max(scores, -1, keepdims=True)
    shifted = jnp.exp2((scores - top) * EXP2_SCALE)
    total = jnp.sum(shifted, -1, keepdims=True)
    summed = jnp.dot(shifted.astype(jnp.bfloat16), values, preferred_element_type=jnp.float32)
    return (summed / total).astype(jnp.bfloat16)


def scores_of(queries, keys):
    return lax.dot_general(
        queries, keys, (((1,), (1,)), ((), ())), preferred_element_type=jnp.float32
    )


def band_kernel(first_ref, q_ref, kp_ref, kc_ref, vp_ref, vc_ref, o_ref):
    has_prev = first_ref[0] + pl.program_id(0) > 0
    for tile in range(COLS // TILE):
        low, high = tile * TILE, (tile + 1) * TILE
        queries = q_ref[low:high, :]
        keys = jnp.concatenate([kp_ref[low:, :], kc_ref[:high, :]], 0)
        values = jnp.concatenate([vp_ref[low:, :], vc_ref[:high, :]], 0)
        scores = scores_of(queries, keys)
        row = lax.broadcasted_iota(jnp.int32, scores.shape, 0)
        col = lax.broadcasted_iota(jnp.int32, scores.shape, 1)
        allowed = (col > row) & (col <= row + COLS) & ((col >= COLS - low) | has_prev)
        scores = jnp.where(allowed, scores, MASKED)
        o_ref[low:high, :] = softmax_values(scores, values)


def band_attention(first, queries, key_prev, key_now, value_prev, value_now, lines, q_at, prev_at, now_at):
    groups = queries.shape[1] // HD

    def block(at):
        return pl.BlockSpec((COLS, HD), lambda line, head, _: (line + at, head))

    return pl.pallas_call(
        band_kernel,
        grid_spec=pltpu.PrefetchScalarGridSpec(
            num_scalar_prefetch=1,
            grid=(lines, groups),
            in_specs=[block(q_at), block(prev_at), block(now_at), block(prev_at), block(now_at)],
            out_specs=block(0),
        ),
        out_shape=jax.ShapeDtypeStruct((lines * COLS, groups * HD), jnp.bfloat16),
        compiler_params=params(2),
        cost_estimate=pl.CostEstimate(
            flops=4 * lines * COLS * 768 * HD * groups,
            bytes_accessed=lines * COLS * groups * HD * 12,
            transcendentals=lines * COLS * 768 * groups,
        ),
        name="band_attention",
    )(first, queries, key_prev, key_now, value_prev, value_now)


def project_kernel(parts, width, *refs):
    row_refs, (own_ref, far_ref, residual_ref, gain_ref, out_ref, normed_ref) = (
        refs[:parts],
        refs[parts:],
    )
    step = pl.program_id(0)
    terms = residual_ref[...].astype(jnp.float32)
    for part in range(parts):
        weight = own_ref[0] if part == 0 else far_ref[0, part - 1]
        terms += jnp.dot(row_refs[part][...], weight, preferred_element_type=jnp.float32)
    out_ref[:, pl.ds(pl.multiple_of(step * width, width), width)] = terms.astype(jnp.bfloat16)

    @pl.when(step == pl.num_programs(0) - 1)
    def _():
        rows = out_ref.shape[0]
        tile = min(rows, 64)

        def norm(at, _):
            here = pl.ds(pl.multiple_of(at * tile, tile), tile)
            stream = out_ref[here, :].astype(jnp.float32)
            center = stream - jnp.mean(stream, -1, keepdims=True)
            variance = jnp.mean(center * center, -1, keepdims=True)
            normed_ref[here, :] = (
                center * lax.rsqrt(variance + EPSILON) * gain_ref[...]
            ).astype(jnp.bfloat16)
            return 0

        lax.fori_loop(0, rows // tile, norm, 0)


def project_and_norm(row_parts, own_weight, far_weight, residual, gain):
    steps, depth, width = own_weight.shape
    parts = len(row_parts)
    rows, features = residual.shape
    whole = pl.BlockSpec((rows, features), lambda i: (0, 0))
    return pl.pallas_call(
        functools.partial(project_kernel, parts, width),
        grid=(steps,),
        in_specs=[pl.BlockSpec((rows, depth), lambda i: (0, 0))] * parts
        + [
            pl.BlockSpec((1, depth, width), lambda i: (i, 0, 0)),
            pl.BlockSpec((1, parts - 1, depth, width), lambda i: (i, 0, 0, 0)),
            pl.BlockSpec((rows, width), lambda i: (0, i)),
            pl.BlockSpec((1, features), lambda i: (0, 0)),
        ],
        out_specs=[whole, whole],
        out_shape=[jax.ShapeDtypeStruct((rows, features), jnp.bfloat16)] * 2,
        compiler_params=params(1),
        cost_estimate=pl.CostEstimate(
            flops=2 * rows * parts * depth * features,
            bytes_accessed=2 * parts * own_weight.size + 6 * rows * features,
            transcendentals=rows,
        ),
        name="project_and_norm",
    )(*row_parts, own_weight, far_weight, residual, gain)


def column_kernel(columns, qkv_ref, o_ref):
    height = qkv_ref.shape[0] // columns
    part = min(qkv_ref.shape[0], 256)
    for low in range(0, height * columns, part):
        high = low + part
        scores = scores_of(qkv_ref[low:high, :HD], qkv_ref[:high, HD : 2 * HD])
        row = lax.broadcasted_iota(jnp.int32, scores.shape, 0) + low
        col = lax.broadcasted_iota(jnp.int32, scores.shape, 1)
        allowed = (col <= row) & (((row - col) & (columns - 1)) == 0)
        scores = jnp.where(allowed, scores, MASKED)
        o_ref[low:high] = softmax_values(scores, qkv_ref[:high, 2 * HD :])


def column_attention(qkv):
    height, columns, features = qkv.shape
    groups = features // (3 * HD)
    attended = pl.pallas_call(
        functools.partial(column_kernel, columns),
        grid=(groups,),
        in_specs=[pl.BlockSpec((height * columns, 3 * HD), lambda g: (0, g))],
        out_specs=pl.BlockSpec((height * columns, HD), lambda g: (0, g)),
        out_shape=jax.ShapeDtypeStruct((height * columns, groups * HD), jnp.bfloat16),
        compiler_params=params(1),
        cost_estimate=pl.CostEstimate(
            flops=4 * height * columns * groups * 256 * HD,
            bytes_accessed=8 * height * columns * groups * HD,
            transcendentals=height * columns * groups * 256,
        ),
        name="column_attention",
    )(qkv.reshape(height * columns, features))
    return attended.reshape(height, columns, groups * HD)


def passed_along(array, axis, by):
    size = lax.axis_size(axis)
    pairs = [(i, i + by) for i in range(size) if 0 <= i + by < size]
    return lax.ppermute(array, axis, pairs)


def from_behind(array, by):
    size = lax.axis_size("head")
    return lax.ppermute(array, "head", [(i, (i + by) % size) for i in range(size)])


def after(value, *others):
    return lax.optimization_barrier((value, *others))[0]


def moved(value, pairs):
    return lax.ppermute(value, "head", pairs)


def line_first(array):
    return (
        moved(array, [(0, 1), (1, 2), (2, 3)]),
        moved(array, [(1, 0), (2, 1), (3, 2)]),
        moved(array, [(0, 3), (3, 0)]),
    )


def line_second(array, below, above, across):
    place = lax.axis_index("head")
    at_end = (place == 0) | (place == 3)
    below_two = moved(below, [(1, 2), (2, 3)])
    above_two = moved(above, [(2, 1), (1, 0)])
    slots = [
        (below, (place + 3) % 4),
        (above, (place + 1) % 4),
        (jnp.where(place < 2, above_two, below_two), (place + 2) % 4),
        (jnp.where(at_end, across, array), jnp.where(at_end, 3 - place, place)),
    ]
    gathered = lax.dynamic_update_index_in_dim(
        jnp.zeros((4, *array.shape), array.dtype), array, place, 0
    )
    for value, slot in slots:
        gathered = lax.dynamic_update_index_in_dim(gathered, value, slot, 0)
    return gathered


def per_device(row_queries, row_keys, row_values, residual_in, out_weight, norm_gain, qkv_weight):
    positions, features = row_queries.shape
    lines = positions // COLS
    seq, heads = lax.axis_size("seq"), lax.axis_size("head")
    place = lax.axis_index("head")
    share, model = residual_in.shape
    gain = norm_gain.reshape(1, model)
    block = min(share, COLS)
    blocks = COLS // block
    half = share // 2

    own_weight = lax.all_gather(out_weight, "seq")
    far_weight = jnp.stack([from_behind(out_weight, by) for by in range(1, heads)])

    key_back, value_back = passed_along((row_keys[-COLS:], row_values[-COLS:]), "seq", 1)
    halves = residual_in.reshape(share // block, 2, block // 2, model)
    residual_own = halves[:, 0].reshape(half, model)
    residual_first = line_second(residual_own, *line_first(residual_own))

    first_row = (lax.axis_index("seq") * lines).reshape(1)
    row_out = [
        band_attention(
            first_row, row_queries, key_back, row_keys, value_back, row_values, 1, 0, 0, 0
        )
    ]
    if lines > 1:
        row_out.append(
            band_attention(
                first_row + 1,
                row_queries,
                row_keys,
                row_keys,
                row_values,
                row_values,
                lines - 1,
                1,
                0,
                1,
            )
        )
    row_out = jnp.concatenate(row_out, 0)
    far_weight = after(far_weight, row_out)
    qkv_own = after(qkv_weight.reshape(qkv_weight.shape[0], -1), far_weight)
    far_weight = lax.all_gather(far_weight, "seq")
    qkv_flat = lax.all_gather(qkv_own, "seq", axis=0, tiled=True)
    row_out = row_out.reshape(heads, share // block, 2, block // 2, features)
    row_first = row_out[:, :, 0].reshape(heads * half, features)
    row_last = row_out[:, :, 1].reshape(heads, half, features)

    parts_first = [row_first] + [from_behind(row_first, by) for by in range(1, heads)]
    parts_last = [
        from_behind(
            lax.dynamic_index_in_dim(row_last, (place + by) % heads, 0, keepdims=False), by
        )
        if by
        else lax.dynamic_index_in_dim(row_last, place, 0, keepdims=False)
        for by in range(heads)
    ]
    out_last, normed_last = project_and_norm(
        parts_last, own_weight, far_weight, halves[:, 1].reshape(half, model), gain
    )
    out_first, normed_first = project_and_norm(
        parts_first, own_weight, far_weight, residual_first.reshape(heads * half, model), gain
    )
    out_first = lax.dynamic_slice_in_dim(out_first, place * half, half, 0)
    copies = line_first(normed_last)
    normed_first = after(normed_first, *copies[:2])
    normed_last = line_second(normed_last, *copies).reshape(heads * half, model)

    def attend(normed):
        own_columns = COLS // 2 // seq
        projected = jnp.dot(normed, qkv_flat, preferred_element_type=jnp.float32)
        qkv = projected.astype(jnp.bfloat16).reshape(lines, seq, own_columns, -1)
        qkv = lax.all_to_all(
            qkv.transpose(1, 0, 2, 3), "seq", split_axis=0, concat_axis=0, tiled=True
        )
        return column_attention(qkv.reshape(seq * lines, own_columns, -1))

    def send_back(attended):
        own_columns = attended.shape[1]
        attended = lax.all_to_all(
            attended.reshape(seq, lines, own_columns, features),
            "seq",
            split_axis=0,
            concat_axis=0,
            tiled=True,
        )
        return attended.transpose(1, 0, 2, 3).reshape(lines, blocks, block // 2, features)

    attended_first = attend(normed_first)
    sent_first = send_back(attended_first)
    attended_last = attend(after(normed_last, attended_first))
    sent_last = send_back(after(attended_last, sent_first))
    column_out = jnp.stack([sent_first, sent_last], 2)
    residual_out = jnp.stack(
        [piece.reshape(share // block, block // 2, model) for piece in (out_first, out_last)], 1
    )
    return residual_out.reshape(share, model), column_out.reshape(positions, features)


def solution(mesh):
    placed = (
        P("seq", "head"),
        P("seq", "head"),
        P("seq", "head"),
        P(("seq", "head"), None),
        P("head", "seq"),
        P(),
        P("seq", "head", None, None),
    )
    return jax.shard_map(
        per_device,
        mesh=mesh,
        in_specs=placed,
        out_specs=(P(("seq", "head"), None), P("seq", "head")),
        check_vma=False,
    )
```

```python
import functools

import jax
import jax.numpy as jnp
from jax import lax
from jax.experimental import pallas as pl
from jax.experimental.pallas import tpu as pltpu
from jax.sharding import PartitionSpec as P

HD = 128
COLS = 512
EPSILON = 1e-05
TILE = 256
EXP2_SCALE = HD ** (-0.5) * 1.4426950408889634
MASKED = -1e30
VMEM = 56 * 1024 * 1024


def params(grid_rank):
    return pltpu.CompilerParams(
        dimension_semantics=("arbitrary",) * grid_rank, vmem_limit_bytes=VMEM
    )


def softmax_values(scores, values):
    top = jnp.max(scores, -1, keepdims=True)
    shifted = jnp.exp2((scores - top) * EXP2_SCALE)
    total = jnp.sum(shifted, -1, keepdims=True)
    summed = jnp.dot(shifted.astype(jnp.bfloat16), values, preferred_element_type=jnp.float32)
    return (summed / total).astype(jnp.bfloat16)


def scores_of(queries, keys):
    return lax.dot_general(
        queries, keys, (((1,), (1,)), ((), ())), preferred_element_type=jnp.float32
    )


def band_kernel(first_ref, q_ref, kp_ref, kc_ref, vp_ref, vc_ref, o_ref):
    has_prev = first_ref[0] + pl.program_id(0) > 0
    for tile in range(COLS // TILE):
        low, high = tile * TILE, (tile + 1) * TILE
        queries = q_ref[low:high, :]
        keys = jnp.concatenate([kp_ref[low:, :], kc_ref[:high, :]], 0)
        values = jnp.concatenate([vp_ref[low:, :], vc_ref[:high, :]], 0)
        scores = scores_of(queries, keys)
        row = lax.broadcasted_iota(jnp.int32, scores.shape, 0)
        col = lax.broadcasted_iota(jnp.int32, scores.shape, 1)
        allowed = (col > row) & (col <= row + COLS) & ((col >= COLS - low) | has_prev)
        scores = jnp.where(allowed, scores, MASKED)
        o_ref[low:high, :] = softmax_values(scores, values)


def band_attention(first, queries, key_prev, key_now, value_prev, value_now, lines, q_at, prev_at, now_at):
    groups = queries.shape[1] // HD

    def block(at):
        return pl.BlockSpec((COLS, HD), lambda line, head, _: (line + at, head))

    return pl.pallas_call(
        band_kernel,
        grid_spec=pltpu.PrefetchScalarGridSpec(
            num_scalar_prefetch=1,
            grid=(lines, groups),
            in_specs=[block(q_at), block(prev_at), block(now_at), block(prev_at), block(now_at)],
            out_specs=block(0),
        ),
        out_shape=jax.ShapeDtypeStruct((lines * COLS, groups * HD), jnp.bfloat16),
        compiler_params=params(2),
        cost_estimate=pl.CostEstimate(
            flops=4 * lines * COLS * 768 * HD * groups,
            bytes_accessed=lines * COLS * groups * HD * 12,
            transcendentals=lines * COLS * 768 * groups,
        ),
        name="band_attention",
    )(first, queries, key_prev, key_now, value_prev, value_now)


def project_kernel(parts, width, *refs):
    row_refs, (own_ref, far_ref, residual_ref, gain_ref, out_ref, normed_ref) = (
        refs[:parts],
        refs[parts:],
    )
    step = pl.program_id(0)
    terms = residual_ref[...].astype(jnp.float32)
    for part in range(parts):
        weight = own_ref[0] if part == 0 else far_ref[0, part - 1]
        terms += jnp.dot(row_refs[part][...], weight, preferred_element_type=jnp.float32)
    out_ref[:, pl.ds(pl.multiple_of(step * width, width), width)] = terms.astype(jnp.bfloat16)

    @pl.when(step == pl.num_programs(0) - 1)
    def _():
        rows = out_ref.shape[0]
        tile = min(rows, 64)

        def norm(at, _):
            here = pl.ds(pl.multiple_of(at * tile, tile), tile)
            stream = out_ref[here, :].astype(jnp.float32)
            center = stream - jnp.mean(stream, -1, keepdims=True)
            variance = jnp.mean(center * center, -1, keepdims=True)
            normed_ref[here, :] = (
                center * lax.rsqrt(variance + EPSILON) * gain_ref[...]
            ).astype(jnp.bfloat16)
            return 0

        lax.fori_loop(0, rows // tile, norm, 0)


def project_and_norm(row_parts, own_weight, far_weight, residual, gain):
    steps, depth, width = own_weight.shape
    parts = len(row_parts)
    rows, features = residual.shape
    whole = pl.BlockSpec((rows, features), lambda i: (0, 0))
    return pl.pallas_call(
        functools.partial(project_kernel, parts, width),
        grid=(steps,),
        in_specs=[pl.BlockSpec((rows, depth), lambda i: (0, 0))] * parts
        + [
            pl.BlockSpec((1, depth, width), lambda i: (i, 0, 0)),
            pl.BlockSpec((1, parts - 1, depth, width), lambda i: (i, 0, 0, 0)),
            pl.BlockSpec((rows, width), lambda i: (0, i)),
            pl.BlockSpec((1, features), lambda i: (0, 0)),
        ],
        out_specs=[whole, whole],
        out_shape=[jax.ShapeDtypeStruct((rows, features), jnp.bfloat16)] * 2,
        compiler_params=params(1),
        cost_estimate=pl.CostEstimate(
            flops=2 * rows * parts * depth * features,
            bytes_accessed=2 * parts * own_weight.size + 6 * rows * features,
            transcendentals=rows,
        ),
        name="project_and_norm",
    )(*row_parts, own_weight, far_weight, residual, gain)


def column_kernel(columns, qkv_ref, o_ref):
    height = qkv_ref.shape[0] // columns
    part = min(qkv_ref.shape[0], 256)
    for low in range(0, height * columns, part):
        high = low + part
        scores = scores_of(qkv_ref[low:high, :HD], qkv_ref[:high, HD : 2 * HD])
        row = lax.broadcasted_iota(jnp.int32, scores.shape, 0) + low
        col = lax.broadcasted_iota(jnp.int32, scores.shape, 1)
        allowed = (col <= row) & (((row - col) & (columns - 1)) == 0)
        scores = jnp.where(allowed, scores, MASKED)
        o_ref[low:high] = softmax_values(scores, qkv_ref[:high, 2 * HD :])


def column_attention(qkv):
    height, columns, features = qkv.shape
    groups = features // (3 * HD)
    attended = pl.pallas_call(
        functools.partial(column_kernel, columns),
        grid=(groups,),
        in_specs=[pl.BlockSpec((height * columns, 3 * HD), lambda g: (0, g))],
        out_specs=pl.BlockSpec((height * columns, HD), lambda g: (0, g)),
        out_shape=jax.ShapeDtypeStruct((height * columns, groups * HD), jnp.bfloat16),
        compiler_params=params(1),
        cost_estimate=pl.CostEstimate(
            flops=4 * height * columns * groups * 256 * HD,
            bytes_accessed=8 * height * columns * groups * HD,
            transcendentals=height * columns * groups * 256,
        ),
        name="column_attention",
    )(qkv.reshape(height * columns, features))
    return attended.reshape(height, columns, groups * HD)


def passed_along(array, axis, by):
    size = lax.axis_size(axis)
    pairs = [(i, i + by) for i in range(size) if 0 <= i + by < size]
    return lax.ppermute(array, axis, pairs)


def from_behind(array, by):
    size = lax.axis_size("head")
    return lax.ppermute(array, "head", [(i, (i + by) % size) for i in range(size)])


def after(value, *others):
    return lax.optimization_barrier((value, *others))[0]


def moved(value, pairs):
    return lax.ppermute(value, "head", pairs)


def line_first(array):
    return moved(array, [(0, 1), (1, 2), (2, 3)]), moved(array, [(1, 0), (2, 1), (3, 2)])


def line_second(array, below, above):
    place = lax.axis_index("head")
    at_end = (place == 0) | (place == 3)
    below_two = moved(below, [(1, 2), (2, 3)])
    above_two = moved(above, [(2, 1), (1, 0)])
    across = moved(array, [(0, 3), (3, 0)])
    slots = [
        (below, (place + 3) % 4),
        (above, (place + 1) % 4),
        (jnp.where(place < 2, above_two, below_two), (place + 2) % 4),
        (jnp.where(at_end, across, array), jnp.where(at_end, 3 - place, place)),
    ]
    gathered = lax.dynamic_update_index_in_dim(
        jnp.zeros((4, *array.shape), array.dtype), array, place, 0
    )
    for value, slot in slots:
        gathered = lax.dynamic_update_index_in_dim(gathered, value, slot, 0)
    return gathered


def per_device(row_queries, row_keys, row_values, residual_in, out_weight, norm_gain, qkv_weight):
    positions, features = row_queries.shape
    lines = positions // COLS
    seq, heads = lax.axis_size("seq"), lax.axis_size("head")
    place = lax.axis_index("head")
    share, model = residual_in.shape
    gain = norm_gain.reshape(1, model)
    block = min(share, COLS)
    blocks = COLS // block
    half = share // 2

    own_weight = lax.all_gather(out_weight, "seq")
    far_weight = jnp.stack([from_behind(out_weight, by) for by in range(1, heads)])

    key_back, value_back = passed_along((row_keys[-COLS:], row_values[-COLS:]), "seq", 1)
    halves = residual_in.reshape(share // block, 2, block // 2, model)
    residual_own = halves[:, 0].reshape(half, model)
    residual_copies = line_first(residual_own)
    residual_first = line_second(residual_own, *residual_copies)

    first_row = (lax.axis_index("seq") * lines).reshape(1)
    row_out = [
        band_attention(
            first_row, row_queries, key_back, row_keys, value_back, row_values, 1, 0, 0, 0
        )
    ]
    if lines > 1:
        row_out.append(
            band_attention(
                first_row + 1,
                row_queries,
                row_keys,
                row_keys,
                row_values,
                row_values,
                lines - 1,
                1,
                0,
                1,
            )
        )
    row_out = jnp.concatenate(row_out, 0)
    far_weight = after(far_weight, row_out, *residual_copies)
    qkv_own = after(qkv_weight.reshape(qkv_weight.shape[0], -1), far_weight)
    far_weight = lax.all_gather(far_weight, "seq")
    qkv_flat = lax.all_gather(qkv_own, "seq", axis=0, tiled=True)
    row_out = row_out.reshape(heads, share // block, 2, block // 2, features)
    row_first = row_out[:, :, 0].reshape(heads * half, features)
    row_last = row_out[:, :, 1].reshape(heads, half, features)

    parts_first = [row_first] + [from_behind(row_first, by) for by in range(1, heads)]
    parts_last = [
        from_behind(
            lax.dynamic_index_in_dim(row_last, (place + by) % heads, 0, keepdims=False), by
        )
        if by
        else lax.dynamic_index_in_dim(row_last, place, 0, keepdims=False)
        for by in range(heads)
    ]
    out_last, normed_last = project_and_norm(
        parts_last, own_weight, far_weight, halves[:, 1].reshape(half, model), gain
    )
    out_first, normed_first = project_and_norm(
        parts_first, own_weight, far_weight, residual_first.reshape(heads * half, model), gain
    )
    out_first = lax.dynamic_slice_in_dim(out_first, place * half, half, 0)
    copies = line_first(normed_last)
    normed_last = line_second(normed_last, *copies).reshape(heads * half, model)

    def attend(normed):
        own_columns = COLS // 2 // seq
        projected = jnp.dot(normed, qkv_flat, preferred_element_type=jnp.float32)
        qkv = projected.astype(jnp.bfloat16).reshape(lines, seq, own_columns, -1)
        qkv = lax.all_to_all(
            qkv.transpose(1, 0, 2, 3), "seq", split_axis=0, concat_axis=0, tiled=True
        )
        return column_attention(qkv.reshape(seq * lines, own_columns, -1))

    def send_back(attended):
        own_columns = attended.shape[1]
        attended = lax.all_to_all(
            attended.reshape(seq, lines, own_columns, features),
            "seq",
            split_axis=0,
            concat_axis=0,
            tiled=True,
        )
        return attended.transpose(1, 0, 2, 3).reshape(lines, blocks, block // 2, features)

    attended_first = attend(normed_first)
    sent_first = send_back(attended_first)
    attended_last = attend(after(normed_last, attended_first))
    sent_last = send_back(after(attended_last, sent_first))
    column_out = jnp.stack([sent_first, sent_last], 2)
    residual_out = jnp.stack(
        [piece.reshape(share // block, block // 2, model) for piece in (out_first, out_last)], 1
    )
    return residual_out.reshape(share, model), column_out.reshape(positions, features)


def solution(mesh):
    placed = (
        P("seq", "head"),
        P("seq", "head"),
        P("seq", "head"),
        P(("seq", "head"), None),
        P("head", "seq"),
        P(),
        P("seq", "head", None, None),
    )
    return jax.shard_map(
        per_device,
        mesh=mesh,
        in_specs=placed,
        out_specs=(P(("seq", "head"), None), P("seq", "head")),
        check_vma=False,
    )
```
